512 devices in a mesh: island: 32 (over y, x), member: 16 (over z, core).
Axes of the slice: x: 4, y: 8, z: 8, core: 2. Of those that a mesh axis runs over, the one named last changes fastest.
Arguments:
- tokens: bfloat16 [32, 2304, 5120], P('island', 'member'), may hold values from -6 to 6
- cotangent: bfloat16 [32, 2048, 768], P('island', 'member'), may hold values from -6 to 6
- slot_token: int32 [32, 2048], P('island', 'member'), may hold values from 0 to 143, as said below
- outer_weight: float32 [5120, 768], P('member', 'island'), may hold values from -5 to 5
- outer_momentum: float32 [5120, 768], P('member', 'island'), may hold values from -2 to 2
- first_moment: float32 [32, 5120, 768], P('island', 'member'), may hold values from -0.4 to 0.4
- second_moment: float32 [32, 5120, 768], P('island', 'member'), may hold values from 0.002 to 0.02
- error_state: bfloat16 [32, 5120, 768], P('island', 'member'), may hold values from -0.3984375 to 0.3984375
Outputs:
- new_outer: float32 [5120, 768], P('member', 'island')
- new_momentum: float32 [5120, 768], P('member', 'island')
The draws below stay inside these ranges and needn't reach their ends.
Inputs may be any that keep to these rules, and one draw needn't show every extreme that they name: `slot_token`: within the 128 slots filled by one member of one replica, the indices are distinct.
All inputs are finite; a program needn't handle non-finite values.
Results may differ from the reference program's by a relative error of at most 0.003.
Values may be sent and summed in bfloat16 or wider, within the bound.
No kernel may reach another device: no remote copies, remote signals or barrier semaphores. Data moves between devices by JAX's collectives and lax.ppermute only.
A program may use at most 64 MiB of HBM per device.

```python
import math
import jax
import jax.numpy as jnp
from jax import lax

D = 5120
FF = 768
SLOT_DEV = 128
TOK_DEV = 144
SLOTS = 2048
TOKENS = 2304
ISLANDS = 32
N_MEMBER = 16


def draw_slot_token(key, part):
    scores = jax.random.randint(key, (ISLANDS, N_MEMBER, TOK_DEV), 0, 2 ** 20)
    ranks = jnp.arange(TOK_DEV, dtype=jnp.int32)
    distinct = scores * TOK_DEV + ranks[None, None, :]
    ordering = jnp.argsort(distinct, axis=2, stable=True).astype(jnp.int32)
    chosen = ordering[:, :, :SLOT_DEV]
    return chosen.reshape((ISLANDS, SLOTS)).astype(jnp.int32)


def with_spikes(drawn, rng, source, target, shards_of, factor):
    def block_of(axis_at):
        return (jnp.arange(drawn.shape[axis_at]) // (drawn.shape[axis_at] // shards_of)).reshape((-1,) + (1,) * (drawn.ndim - 1 - axis_at))

    one_side = jax.random.permutation(rng, shards_of)[block_of(target)]
    second = (block_of(target) + shards_of // 2) % shards_of
    return jnp.where((block_of(source) == one_side) | (block_of(source) == second), factor * drawn, drawn)


def block_levels(stream_key, shape, cuts, low, high):
    level = 1.0
    for position, parts in cuts:
        steps = jax.random.uniform(jax.random.fold_in(jax.random.fold_in(stream_key, 6), position), (parts,), jnp.float32, low / len(cuts), high / len(cuts))
        level = level * jnp.repeat(jnp.exp(steps), shape[position] // parts).reshape((-1,) + (1,) * (len(shape) - 1 - position))
    return level


def gaussian(stream_key, extent, spread, bound, shards=(), kind=jnp.bfloat16):
    array = spread * jax.random.normal(stream_key, extent, jnp.float32)
    if shards:
        array = array * block_levels(stream_key, extent, shards, -0.22, 0.18)
    return jnp.clip(array, -bound, bound).astype(kind)


def noise_with(rng, extent, spread, limit, pieces, heavy, kind=jnp.bfloat16):
    drawn = spread * jax.random.normal(rng, extent, jnp.float32)
    if pieces:
        drawn = drawn * block_levels(rng, extent, pieces, -0.22, 0.18)
    return jnp.clip(with_spikes(drawn, jax.random.fold_in(rng, 3), *heavy), -limit, limit).astype(kind)


def setup_inputs(seed: int = 0) -> dict:
    seeds = jax.random.split(jax.random.key(seed), 9)
    tokens = gaussian(seeds[0], (ISLANDS, TOKENS, D), 1.0, 6.0, ((0, 32), (1, 16)))
    cotangent = noise_with(seeds[1], (ISLANDS, SLOTS, FF), 1.0, 6.0, ((0, 32), (1, 16)), (0, 2, 32, 2.75))
    slot_token = draw_slot_token(jax.random.fold_in(seeds[8], 71), 0)
    outer_weight = gaussian(seeds[3], (D, FF), 1.0, 5.0, ((0, 16), (1, 32)), jnp.float32)
    outer_momentum = gaussian(seeds[4], (D, FF), 0.3, 2.0, ((0, 16), (1, 32)), jnp.float32)
    first_moment = gaussian(seeds[5], (ISLANDS, D, FF), 0.05, 0.4, ((0, 32), (1, 16)), jnp.float32)
    second_moment = jnp.clip(jnp.exp(math.log(0.02) - 2.30258502 * jax.random.uniform(seeds[6], (ISLANDS, D, FF), jnp.float32) ** block_levels(seeds[6], (ISLANDS, D, FF), ((0, 32), (1, 16)), -0.2, 0.2)), 0.002, 0.02)
    error_state = noise_with(seeds[7], (ISLANDS, D, FF), 0.05, 0.3984375, ((0, 32), (1, 16)), (0, 2, 32, 2.75))
    return dict(tokens=tokens, cotangent=cotangent, slot_token=slot_token, outer_weight=outer_weight, outer_momentum=outer_momentum, first_moment=first_moment, second_moment=second_moment, error_state=error_state)


def silu_grad(values):
    sigmoid = jax.nn.sigmoid(values)
    return sigmoid * (1.0 + values * (1.0 - sigmoid))

def reference(tokens, cotangent, slot_token, outer_weight, outer_momentum, first_moment, second_moment, error_state):
    fan_scale = float(D) ** (-0.5)
    weight_low = outer_weight.astype(jnp.bfloat16)
    rows_member = D // N_MEMBER
    offsets = (jnp.arange(SLOTS) // SLOT_DEV * TOK_DEV).astype(jnp.int32)

    def island_step(summed, inputs):
        island_tokens, island_cot, island_slots, moment_old, square_old, island_error = inputs
        routed = jnp.take(island_tokens, offsets + island_slots.astype(jnp.int32), axis=0)
        pre_act = jnp.zeros((SLOTS, FF), jnp.float32)
        for member in range(N_MEMBER):
            columns = routed[:, member * rows_member:(member + 1) * rows_member]
            weight_rows = weight_low[member * rows_member:(member + 1) * rows_member, :]
            part_low = (jnp.dot(columns, weight_rows, preferred_element_type=jnp.float32) * fan_scale).astype(jnp.bfloat16)
            pre_act = pre_act + lax.optimization_barrier(part_low).astype(jnp.float32)
        hidden_grad = (island_cot.astype(jnp.float32) * silu_grad(pre_act)).astype(jnp.bfloat16)
        inner_grad = jnp.dot(routed.T, hidden_grad, preferred_element_type=jnp.float32) * fan_scale
        moment_one = 0.9 * moment_old + 0.1 * inner_grad
        moment_two = 0.95 * square_old + 0.05 * inner_grad * inner_grad
        pseudo_grad = 0.25 * (moment_one / (jnp.sqrt(moment_two) + 1e-08) + 0.1 * outer_weight)
        compressed = (pseudo_grad + island_error.astype(jnp.float32)).astype(jnp.bfloat16)
        return (summed + compressed.astype(jnp.float32), None)
    summed, unused = lax.scan(island_step, jnp.zeros((D, FF), jnp.float32), (tokens, cotangent, slot_token, first_moment, second_moment, error_state))
    averaged = summed / float(ISLANDS)
    new_momentum = 0.9 * outer_momentum + averaged
    new_outer = outer_weight - 0.7 * (averaged + 0.9 * new_momentum)
    return (new_outer, new_momentum)
```

```python
import jax
import jax.numpy as jnp
from jax import lax
from jax.experimental import pallas as pl
from jax.experimental.pallas import tpu as pltpu
from jax.sharding import PartitionSpec as P

NY, NX, NM = 8, 4, 16
ALONG_X = [[y * NX + x for x in range(NX)] for y in range(NY)]
ALONG_Y = [[y * NX + x for y in range(NY)] for x in range(NX)]
BF = jnp.bfloat16
F32 = jnp.float32


def spread(block, groups):
    n = len(groups[0])
    return lax.all_to_all(
        jnp.broadcast_to(block[None], (n,) + block.shape),
        "island",
        split_axis=0,
        concat_axis=0,
        tiled=True,
        axis_index_groups=groups,
    )


def hidden_kernel(scale, x_ref, w_ref, cot_ref, out_ref, acc_ref):
    step = pl.program_id(0)
    total = None
    for m in range(x_ref.shape[0]):
        part = lax.dot_general(
            x_ref[m], w_ref[m], (((0,), (0,)), ((), ())), preferred_element_type=F32
        )
        total = part if total is None else total + part

    @pl.when(step == 0)
    def _():
        acc_ref[...] = total

    @pl.when(step > 0)
    def _():
        acc_ref[...] += total

    @pl.when(step == pl.num_programs(0) - 1)
    def _():
        pre = acc_ref[...] * scale
        sig = 1.0 / (1.0 + jnp.exp(-pre))
        grad = sig * (1.0 + pre * (1.0 - sig))
        out_ref[...] = (cot_ref[...].astype(F32) * grad).astype(BF)


def hidden(xt, w, cot, scale):
    nm, rows, slots = xt.shape
    ff = w.shape[2]
    per = 2
    return pl.pallas_call(
        lambda *refs: hidden_kernel(scale, *refs),
        grid=(nm // per,),
        in_specs=[
            pl.BlockSpec((per, rows, slots), lambda i: (i, 0, 0)),
            pl.BlockSpec((per, rows, ff), lambda i: (i, 0, 0)),
            pl.BlockSpec((slots, ff), lambda i: (0, 0)),
        ],
        out_specs=pl.BlockSpec((slots, ff), lambda i: (0, 0)),
        out_shape=jax.ShapeDtypeStruct((slots, ff), BF),
        scratch_shapes=[pltpu.VMEM((slots, ff), F32)],
        compiler_params=pltpu.CompilerParams(vmem_limit_bytes=24 * 2**20),
        cost_estimate=pl.CostEstimate(
            flops=2 * nm * rows * slots * ff,
            bytes_accessed=2 * (xt.size + w.size + 2 * cot.size),
            transcendentals=cot.size,
        ),
        name="hidden",
    )(xt, w, cot)


def step_kernel(scale, x_ref, h_ref, m1_ref, m2_ref, err_ref, out_ref):
    total = None
    for m in range(0, x_ref.shape[0], 2):
        left = jnp.concatenate([x_ref[m], x_ref[m + 1]], axis=1)
        right = jnp.concatenate([h_ref[m], h_ref[m + 1]], axis=0)
        part = jnp.dot(left, right, preferred_element_type=F32)
        total = part if total is None else total + part
    grad = total * scale
    one = 0.9 * m1_ref[...] + 0.1 * grad
    two = 0.95 * m2_ref[...] + 0.05 * grad * grad
    moved = 0.25 * (one / (jnp.sqrt(two) + 1e-08)) + err_ref[...].astype(F32)
    out_ref[...] = moved.T.astype(BF)


def inner_step(xt, h, m1, m2, err, scale):
    nm, rows, slots = xt.shape
    ff = h.shape[2]
    blk = 256
    return pl.pallas_call(
        lambda *refs: step_kernel(scale, *refs),
        grid=(ff // blk,),
        in_specs=[
            pl.BlockSpec((nm, rows, slots), lambda i: (0, 0, 0)),
            pl.BlockSpec((nm, slots, blk), lambda i: (0, 0, i)),
            pl.BlockSpec((rows, blk), lambda i: (0, i)),
            pl.BlockSpec((rows, blk), lambda i: (0, i)),
            pl.BlockSpec((rows, blk), lambda i: (0, i)),
        ],
        out_specs=pl.BlockSpec((blk, rows), lambda i: (i, 0)),
        out_shape=jax.ShapeDtypeStruct((ff, rows), BF),
        compiler_params=pltpu.CompilerParams(vmem_limit_bytes=24 * 2**20),
        cost_estimate=pl.CostEstimate(
            flops=2 * nm * rows * slots * ff,
            bytes_accessed=2 * (xt.size + h.size) + 12 * rows * ff,
            transcendentals=2 * rows * ff,
        ),
        name="inner_step",
    )(xt, h, m1, m2, err)


def local(
    tokens,
    cotangent,
    slot_token,
    outer_weight,
    outer_momentum,
    first_moment,
    second_moment,
    error_state,
):
    dim = tokens.shape[2]
    scale = float(dim) ** (-0.5)
    rows, cols = outer_weight.shape
    slots = slot_token.shape[1]
    weight_t = outer_weight.T

    low = weight_t.astype(BF)
    block = spread(low, ALONG_Y).reshape(NY * cols, rows)
    block = spread(block, ALONG_X).reshape(NX, NY, cols, rows)
    block = block.transpose(1, 0, 2, 3).reshape(NX * NY * cols, rows).T
    weights = lax.all_gather(block, "member", axis=0, tiled=False)

    chosen = lax.broadcasted_iota(jnp.int32, (tokens.shape[1], slots), 0) == slot_token
    picked = lax.dot_general(
        tokens[0],
        chosen.astype(BF),
        (((0,), (0,)), ((), ())),
        preferred_element_type=F32,
    ).astype(BF)
    picked = picked.reshape(NM, rows, slots)

    hid = hidden(picked, weights, cotangent[0], scale)
    picked, hid = lax.optimization_barrier((picked, hid))
    routed = lax.all_to_all(picked, "member", split_axis=0, concat_axis=0, tiled=True)
    hid_all = lax.all_gather(hid, "member", axis=0, tiled=False)
    moved = inner_step(
        routed, hid_all, first_moment[0], second_moment[0], error_state[0], scale
    )
    parts = lax.all_to_all(
        moved.reshape(NX * NY, cols, rows), "island", split_axis=0, concat_axis=0, tiled=True
    )
    averaged = jnp.sum(parts.astype(F32), axis=0) / float(NX * NY) + 0.025 * weight_t
    new_momentum = 0.9 * outer_momentum.T + averaged
    new_outer = weight_t - 0.7 * (averaged + 0.9 * new_momentum)
    return (new_outer.T, new_momentum.T)


def solution(mesh):
    in_specs = (
        P("island", "member", None),
        P("island", "member", None),
        P("island", "member"),
        P("member", "island"),
        P("member", "island"),
        P("island", "member", None),
        P("island", "member", None),
        P("island", "member", None),
    )
    out_specs = (P("member", "island"), P("member", "island"))
    return jax.shard_map(local, mesh=mesh, in_specs=in_specs, out_specs=out_specs, check_vma=False)
```

```python
import jax
import jax.numpy as jnp
from jax import lax
from jax.experimental import pallas as pl
from jax.experimental.pallas import tpu as pltpu
from jax.sharding import PartitionSpec as P

NY, NX, NA = 8, 4, 4
ALONG_X = [[y * NX + x for x in range(NX)] for y in range(NY)]
ALONG_Y = [[y * NX + x for y in range(NY)] for x in range(NX)]
TEAM = [[4 * a + 2 * q + c for a in range(NA) for c in range(2)] for q in range(2)]
SAME_CORE = [[4 * a + 2 * q + c for a in range(NA)] for q in range(2) for c in range(2)]
MEMBERS = 4 * NA
BF = jnp.bfloat16
F32 = jnp.float32
VMEM = 16 * 2**20


def swap(x, bit):
    return lax.ppermute(x, "member", [(m, m ^ bit) for m in range(MEMBERS)])


def exchange(x, groups):
    return lax.all_to_all(
        x, "member", split_axis=0, concat_axis=0, tiled=True, axis_index_groups=groups
    )


def parts_kernel(which_ref, x_ref, w_ref, out_ref):
    out_ref[0] = jnp.dot(w_ref[...], x_ref[0, 0], preferred_element_type=F32).astype(BF)


def parts(which, routed, weights):
    na, _, depth, slots = routed.shape
    ff = weights.shape[0]
    return pl.pallas_call(
        parts_kernel,
        grid_spec=pltpu.PrefetchScalarGridSpec(
            num_scalar_prefetch=1,
            grid=(na,),
            in_specs=[
                pl.BlockSpec((1, 1, depth, slots), lambda i, which: (i, which[0], 0, 0)),
                pl.BlockSpec((ff, depth), lambda i, which: (0, 0)),
            ],
            out_specs=pl.BlockSpec((1, ff, slots), lambda i, which: (i, 0, 0)),
        ),
        out_shape=jax.ShapeDtypeStruct((na, ff, slots), BF),
        compiler_params=pltpu.CompilerParams(vmem_limit_bytes=VMEM),
        cost_estimate=pl.CostEstimate(
            flops=2 * na * ff * depth * slots,
            bytes_accessed=2 * (na * depth * slots + ff * depth + na * ff * slots),
            transcendentals=0,
        ),
        name="parts",
    )(which, routed, weights)


def hidden_kernel(scale, p_ref, cot_ref, out_ref):
    total = p_ref[0].astype(F32)
    for a in range(1, p_ref.shape[0]):
        total += p_ref[a].astype(F32)
    pre = total.T * scale
    sig = 1.0 / (1.0 + jnp.exp(-pre))
    grad = sig * (1.0 + pre * (1.0 - sig))
    hid = (cot_ref[...].astype(F32) * grad).astype(BF)
    for a in range(out_ref.shape[0]):
        out_ref[a] = hid


def hidden(partial, cot, scale):
    na, ff, slots = partial.shape
    blk = 256
    return pl.pallas_call(
        lambda *refs: hidden_kernel(scale, *refs),
        grid=(ff // blk,),
        in_specs=[
            pl.BlockSpec((na, blk, slots), lambda i: (0, i, 0)),
            pl.BlockSpec((slots, blk), lambda i: (0, i)),
        ],
        out_specs=pl.BlockSpec((na, slots, blk), lambda i: (0, 0, i)),
        out_shape=jax.ShapeDtypeStruct((na, slots, ff), BF),
        compiler_params=pltpu.CompilerParams(vmem_limit_bytes=VMEM),
        name="hidden",
    )(partial, cot)


def grad_kernel(which_ref, xm_ref, xo_ref, hm_ref, ho_ref, out_ref, acc_ref):
    step = pl.program_id(0)
    left = jnp.concatenate([xm_ref[0, 0, 0], xo_ref[0, 0, 0]], axis=1)
    right = jnp.concatenate([hm_ref[0], ho_ref[0]], axis=0)
    part = jnp.dot(left, right, preferred_element_type=F32)

    @pl.when(step == 0)
    def _():
        acc_ref[...] = part

    @pl.when(step > 0)
    def _():
        acc_ref[...] += part

    @pl.when(step == pl.num_programs(0) - 1)
    def _():
        out_ref[...] = acc_ref[...].astype(out_ref.dtype)


def team_grad(which, block, routed, hid_mine, hid_other, dtype):
    na, _, _, rows, slots = routed.shape
    ff = hid_mine.shape[2]
    return pl.pallas_call(
        grad_kernel,
        grid_spec=pltpu.PrefetchScalarGridSpec(
            num_scalar_prefetch=1,
            grid=(na,),
            in_specs=[
                pl.BlockSpec((1, 1, 1, rows, slots), lambda i, w: (i, w[0], block, 0, 0)),
                pl.BlockSpec((1, 1, 1, rows, slots), lambda i, w: (i, 1 - w[0], block, 0, 0)),
                pl.BlockSpec((1, slots, ff), lambda i, w: (i, 0, 0)),
                pl.BlockSpec((1, slots, ff), lambda i, w: (i, 0, 0)),
            ],
            out_specs=pl.BlockSpec((rows, ff), lambda i, w: (0, 0)),
            scratch_shapes=[pltpu.VMEM((rows, ff), F32)],
        ),
        out_shape=jax.ShapeDtypeStruct((rows, ff), dtype),
        compiler_params=pltpu.CompilerParams(vmem_limit_bytes=VMEM),
        cost_estimate=pl.CostEstimate(
            flops=4 * na * rows * slots * ff,
            bytes_accessed=4 * na * slots * (rows + ff) + 4 * rows * ff,
            transcendentals=0,
        ),
        name="team_grad",
    )(which, routed, routed, hid_mine, hid_other)


def step_kernel(scale, own_ref, far_ref, m1_ref, m2_ref, err_ref, out_ref):
    grad = (own_ref[...] + far_ref[...].astype(F32)) * scale
    one = 0.9 * m1_ref[...] + 0.1 * grad
    two = 0.95 * m2_ref[...] + 0.05 * grad * grad
    moved = 0.25 * (one / (jnp.sqrt(two) + 1e-08)) + err_ref[...].astype(F32)
    out_ref[...] = moved.T.astype(BF)


def inner_step(own, far, m1, m2, err, scale):
    rows, ff = own.shape
    blk = 256
    spec = pl.BlockSpec((rows, blk), lambda i: (0, i))
    return pl.pallas_call(
        lambda *refs: step_kernel(scale, *refs),
        grid=(ff // blk,),
        in_specs=[spec] * 5,
        out_specs=pl.BlockSpec((blk, rows), lambda i: (i, 0)),
        out_shape=jax.ShapeDtypeStruct((ff, rows), BF),
        compiler_params=pltpu.CompilerParams(vmem_limit_bytes=VMEM),
        name="inner_step",
    )(own, far, m1, m2, err)


def local(
    tokens,
    cotangent,
    slot_token,
    outer_weight,
    outer_momentum,
    first_moment,
    second_moment,
    error_state,
):
    scale = float(tokens.shape[2]) ** (-0.5)
    rows, cols = outer_weight.shape
    slots = slot_token.shape[1]
    weight_t = outer_weight.T
    member = lax.axis_index("member")
    core = member & 1
    q = (member >> 1) & 1
    mine = core.astype(jnp.int32).reshape(1)
    other = 1 - mine

    chosen = lax.broadcasted_iota(jnp.int32, (tokens.shape[1], slots), 0) == slot_token
    picked = lax.dot_general(
        tokens[0],
        chosen.astype(BF),
        (((0,), (0,)), ((), ())),
        preferred_element_type=F32,
    ).astype(BF)
    picked = picked.reshape(NA, 2, 2, rows, slots)
    near = lax.dynamic_index_in_dim(picked, q, axis=1, keepdims=False)
    far = lax.dynamic_index_in_dim(picked, 1 - q, axis=1, keepdims=False)
    picked = jnp.stack([near, far], axis=2).reshape(2 * NA, 2 * rows, slots)
    low = weight_t.astype(BF)
    low = jnp.concatenate([low, swap(low, 2)], axis=1)
    picked, low = lax.optimization_barrier((picked, low))
    routed = exchange(picked, TEAM).reshape(NA, 2, 2 * rows, slots)
    low = lax.all_gather(low, "island", axis=0, tiled=True, axis_index_groups=ALONG_X)
    weights = lax.all_gather(low, "island", axis=0, tiled=True, axis_index_groups=ALONG_Y)

    sent = swap(parts(other, routed, weights), 1)
    kept = parts(mine, routed, weights)
    summed = (kept.astype(F32) + sent.astype(F32)).astype(BF)
    hid = hidden(exchange(summed, SAME_CORE), cotangent[0], scale)
    hid_mine = exchange(hid, SAME_CORE)
    hid_other = swap(hid_mine, 1)

    routed = routed.reshape(NA, 2, 2, rows, slots)
    far = swap(team_grad(mine, 1, routed, hid_mine, hid_other, BF), 2)
    own = team_grad(mine, 0, routed, hid_mine, hid_other, F32)
    moved = inner_step(own, far, first_moment[0], second_moment[0], error_state[0], scale)
    shares = lax.all_to_all(
        moved.reshape(NX * NY, cols, rows), "island", split_axis=0, concat_axis=0, tiled=True
    )
    averaged = jnp.sum(shares.astype(F32), axis=0) / float(NX * NY) + 0.025 * weight_t
    new_momentum = 0.9 * outer_momentum.T + averaged
    new_outer = weight_t - 0.7 * (averaged + 0.9 * new_momentum)
    return (new_outer.T, new_momentum.T)


def solution(mesh):
    in_specs = (
        P("island", "member", None),
        P("island", "member", None),
        P("island", "member"),
        P("member", "island"),
        P("member", "island"),
        P("island", "member", None),
        P("island", "member", None),
        P("island", "member", None),
    )
    out_specs = (P("member", "island"), P("member", "island"))
    return jax.shard_map(local, mesh=mesh, in_specs=in_specs, out_specs=out_specs, check_vma=False)
```

```python
import jax
import jax.numpy as jnp
from jax import lax
from jax.experimental import pallas as pl
from jax.experimental.pallas import tpu as pltpu
from jax.sharding import PartitionSpec as P

NY, NX, NA = 8, 4, 4
ALONG_X = [[y * NX + x for x in range(NX)] for y in range(NY)]
TEAM = [[4 * a + 2 * q + c for a in range(NA) for c in range(2)] for q in range(2)]
SAME_CORE = [[4 * a + 2 * q + c for a in range(NA)] for q in range(2) for c in range(2)]
MEMBERS = 4 * NA
BF = jnp.bfloat16
F32 = jnp.float32
VMEM = 16 * 2**20
PACKED = 64


def swap(x, bit):
    return lax.ppermute(x, "member", [(m, m ^ bit) for m in range(MEMBERS)])


def exchange(x, groups):
    return lax.all_to_all(
        x, "member", split_axis=0, concat_axis=0, tiled=True, axis_index_groups=groups
    )


def pick_kernel(q_ref, tok_ref, slot_ref, out_ref):
    shape = (tok_ref.shape[0], slot_ref.shape[1])
    chosen = (lax.broadcasted_iota(jnp.int32, shape, 0) == slot_ref[...]).astype(BF)
    got = lax.dot_general(
        tok_ref[...], chosen, (((0,), (0,)), ((), ())), preferred_element_type=F32
    )
    out_ref[...] = got.astype(BF).reshape(out_ref.shape)


def pick(q, tokens, slot_token, rows):
    slots = slot_token.shape[1]
    return pl.pallas_call(
        pick_kernel,
        grid_spec=pltpu.PrefetchScalarGridSpec(
            num_scalar_prefetch=1,
            grid=(NA, 2),
            in_specs=[
                pl.BlockSpec(
                    (tokens.shape[0], 2 * rows),
                    lambda i, j, q: (0, 2 * i + q[0] + j - 2 * q[0] * j),
                ),
                pl.BlockSpec((1, slots), lambda i, j, q: (0, 0)),
            ],
            out_specs=pl.BlockSpec((1, 2, 1, rows, slots), lambda i, j, q: (i, 0, j, 0, 0)),
        ),
        out_shape=jax.ShapeDtypeStruct((NA, 2, 2, rows, slots), BF),
        compiler_params=pltpu.CompilerParams(vmem_limit_bytes=VMEM),
        name="pick",
    )(q, tokens, slot_token).reshape(2 * NA, 2 * rows, slots)


def parts_kernel(which_ref, x_ref, w_ref, out_ref):
    out_ref[0] = jnp.dot(w_ref[...], x_ref[0, 0], preferred_element_type=F32).astype(BF)


def parts(which, routed, weights):
    na, _, depth, slots = routed.shape
    ff = weights.shape[0]
    return pl.pallas_call(
        parts_kernel,
        grid_spec=pltpu.PrefetchScalarGridSpec(
            num_scalar_prefetch=1,
            grid=(na,),
            in_specs=[
                pl.BlockSpec((1, 1, depth, slots), lambda i, which: (i, which[0], 0, 0)),
                pl.BlockSpec((ff, depth), lambda i, which: (0, 0)),
            ],
            out_specs=pl.BlockSpec((1, ff, slots), lambda i, which: (i, 0, 0)),
        ),
        out_shape=jax.ShapeDtypeStruct((na, ff, slots), BF),
        compiler_params=pltpu.CompilerParams(vmem_limit_bytes=VMEM),
        cost_estimate=pl.CostEstimate(
            flops=2 * na * ff * depth * slots,
            bytes_accessed=2 * (na * depth * slots + ff * depth + na * ff * slots),
            transcendentals=0,
        ),
        name="parts",
    )(which, routed, weights)


def hidden_kernel(scale, p_ref, cot_ref, out_ref):
    total = p_ref[0].astype(F32)
    for a in range(1, p_ref.shape[0]):
        total += p_ref[a].astype(F32)
    ff, slots = total.shape
    total = total.reshape(NX, NY, ff // (NX * NY), slots)
    total = jnp.concatenate([total[x, y] for y in range(NY) for x in range(NX)], axis=0)
    pre = total.T * scale
    sig = 1.0 / (1.0 + jnp.exp(-pre))
    grad = sig * (1.0 + pre * (1.0 - sig))
    hid = (cot_ref[...].astype(F32) * grad).astype(BF)
    for a in range(out_ref.shape[0]):
        out_ref[a] = hid


def hidden(partial, cot, scale):
    na, ff, slots = partial.shape
    return pl.pallas_call(
        lambda *refs: hidden_kernel(scale, *refs),
        in_specs=[pl.BlockSpec(memory_space=pltpu.VMEM)] * 2,
        out_specs=pl.BlockSpec(memory_space=pltpu.VMEM),
        out_shape=jax.ShapeDtypeStruct((na, slots, ff), BF),
        compiler_params=pltpu.CompilerParams(vmem_limit_bytes=VMEM),
        name="hidden",
    )(partial, cot)


def grad_kernel(which_ref, xm_ref, xo_ref, hm_ref, ho_ref, out_ref, acc_ref):
    step = pl.program_id(0)
    left = jnp.concatenate([xm_ref[0, 0, 0], xo_ref[0, 0, 0]], axis=1)
    right = jnp.concatenate([hm_ref[0], ho_ref[0]], axis=0)
    part = jnp.dot(left, right, preferred_element_type=F32)

    @pl.when(step == 0)
    def _():
        acc_ref[...] = part

    @pl.when(step > 0)
    def _():
        acc_ref[...] += part

    @pl.when(step == pl.num_programs(0) - 1)
    def _():
        out_ref[...] = acc_ref[...].astype(out_ref.dtype)


def team_grad(which, block, routed, hid_mine, hid_other, dtype):
    na, _, _, rows, slots = routed.shape
    ff = hid_mine.shape[2]
    return pl.pallas_call(
        grad_kernel,
        grid_spec=pltpu.PrefetchScalarGridSpec(
            num_scalar_prefetch=1,
            grid=(na,),
            in_specs=[
                pl.BlockSpec((1, 1, 1, rows, slots), lambda i, w: (i, w[0], block, 0, 0)),
                pl.BlockSpec((1, 1, 1, rows, slots), lambda i, w: (i, 1 - w[0], block, 0, 0)),
                pl.BlockSpec((1, slots, ff), lambda i, w: (i, 0, 0)),
                pl.BlockSpec((1, slots, ff), lambda i, w: (i, 0, 0)),
            ],
            out_specs=pl.BlockSpec((rows, ff), lambda i, w: (0, 0)),
            scratch_shapes=[pltpu.VMEM((rows, ff), F32)],
        ),
        out_shape=jax.ShapeDtypeStruct((rows, ff), dtype),
        compiler_params=pltpu.CompilerParams(vmem_limit_bytes=VMEM),
        cost_estimate=pl.CostEstimate(
            flops=4 * na * rows * slots * ff,
            bytes_accessed=4 * na * slots * (rows + ff) + 4 * rows * ff,
            transcendentals=0,
        ),
        name="team_grad",
    )(which, routed, routed, hid_mine, hid_other)


def pack(x):
    tail = x[:, :, 256:]
    pad = jnp.zeros_like(tail[:, :8])
    return jnp.concatenate(
        [
            x[:, :, :128],
            x[:, :, 128:256],
            jnp.concatenate([tail[:, :8], tail[:, 8:16]], axis=2),
            jnp.concatenate([tail[:, 16:], pad], axis=2),
        ],
        axis=1,
    )


def unpack(x):
    tail = jnp.concatenate([x[48:56, :64], x[48:56, 64:], x[56:, :64]], axis=0)
    return jnp.concatenate([x[:24], x[24:48], tail], axis=1)


def step_kernel(scale, cols, own_ref, far_ref, m1_ref, m2_ref, err_ref, out_ref):
    grad = (own_ref[...] + far_ref[...].astype(F32)) * scale
    one = 0.9 * m1_ref[...] + 0.1 * grad
    two = 0.95 * m2_ref[...] + 0.05 * grad * grad
    moved = 0.25 * (one / (jnp.sqrt(two) + 1e-08)) + err_ref[...].astype(F32)
    out_ref[...] = pack(moved.T.reshape(-1, cols, moved.shape[0])).astype(BF)


def inner_step(own, far, m1, m2, err, scale, cols):
    rows, ff = own.shape
    blk = ff // 2
    spec = pl.BlockSpec((rows, blk), lambda i: (0, i))
    return pl.pallas_call(
        lambda *refs: step_kernel(scale, cols, *refs),
        grid=(ff // blk,),
        in_specs=[spec] * 5,
        out_specs=pl.BlockSpec((blk // cols, PACKED, 128), lambda i: (i, 0, 0)),
        out_shape=jax.ShapeDtypeStruct((ff // cols, PACKED, 128), BF),
        compiler_params=pltpu.CompilerParams(vmem_limit_bytes=VMEM),
        name="inner_step",
    )(own, far, m1, m2, err)


def local(
    tokens,
    cotangent,
    slot_token,
    outer_weight,
    outer_momentum,
    first_moment,
    second_moment,
    error_state,
):
    scale = float(tokens.shape[2]) ** (-0.5)
    rows, cols = outer_weight.shape
    slots = slot_token.shape[1]
    weight_t = outer_weight.T
    member = lax.axis_index("member")
    core = member & 1
    q = (member >> 1) & 1
    mine = core.astype(jnp.int32).reshape(1)
    other = 1 - mine

    picked = pick(q.reshape(1), tokens[0], slot_token, rows)

    low = weight_t.astype(BF)
    low = jnp.concatenate([low, swap(low, 2)], axis=1)
    picked, low = lax.optimization_barrier((picked, low))
    near = lax.ppermute(low, "island", [(i, i ^ NX) for i in range(NX * NY)])
    routed = exchange(picked, TEAM).reshape(NA, 2, 2 * rows, slots)
    y = lax.axis_index("island") >> 2
    odd = (y & 1) == 1
    pair = jnp.where(odd, jnp.stack([near, low]), jnp.stack([low, near]))
    ring = [pair] + [
        lax.ppermute(
            pair,
            "island",
            [(i, (i + 2 * NX * k) % (NX * NY)) for i in range(NX * NY)],
        )
        for k in (1, 2, 3)
    ]
    ring = jnp.stack([ring[k] for k in (0, 3, 2, 1, 0, 3, 2, 1)])
    column = lax.dynamic_slice_in_dim(ring, (4 - (y >> 1)) & 3, 4, axis=0)
    weights = lax.all_gather(
        column.reshape(NY * cols, 2 * rows), "island", axis=0, tiled=True, axis_index_groups=ALONG_X
    )

    sent = swap(parts(other, routed, weights), 1)
    kept = parts(mine, routed, weights)
    summed = (kept.astype(F32) + sent.astype(F32)).astype(BF)
    hid = hidden(exchange(summed, SAME_CORE), cotangent[0], scale)
    hid_mine = exchange(hid, SAME_CORE)
    hid_other = swap(hid_mine, 1)

    routed = routed.reshape(NA, 2, 2, rows, slots)
    far = swap(team_grad(mine, 1, routed, hid_mine, hid_other, BF), 2)
    own = team_grad(mine, 0, routed, hid_mine, hid_other, F32)
    moved = inner_step(own, far, first_moment[0], second_moment[0], error_state[0], scale, cols)
    shares = lax.all_to_all(
        moved, "island", split_axis=0, concat_axis=0, tiled=True
    )
    averaged = unpack(jnp.sum(shares.astype(F32), axis=0)) / float(NX * NY) + 0.025 * weight_t
    new_momentum = 0.9 * outer_momentum.T + averaged
    new_outer = weight_t - 0.7 * (averaged + 0.9 * new_momentum)
    return (new_outer.T, new_momentum.T)


def solution(mesh):
    in_specs = (
        P("island", "member", None),
        P("island", "member", None),
        P("island", "member"),
        P("member", "island"),
        P("member", "island"),
        P("island", "member", None),
        P("island", "member", None),
        P("island", "member", None),
    )
    out_specs = (P("member", "island"), P("member", "island"))
    return jax.shard_map(local, mesh=mesh, in_specs=in_specs, out_specs=out_specs, check_vma=False)
```

```python
import jax
import jax.numpy as jnp
from jax import lax
from jax.experimental import pallas as pl
from jax.experimental.pallas import tpu as pltpu
from jax.sharding import PartitionSpec as P

NY, NX, NA = 8, 4, 4
ALONG_X = [[y * NX + x for x in range(NX)] for y in range(NY)]
TEAM = [[4 * a + 2 * q + c for a in range(NA) for c in range(2)] for q in range(2)]
SAME_CORE = [[4 * a + 2 * q + c for a in range(NA)] for q in range(2) for c in range(2)]
MEMBERS = 4 * NA
BF = jnp.bfloat16
F32 = jnp.float32
VMEM = 16 * 2**20
PACKED = 64


def swap(x):
    return lax.ppermute(x, "member", [(m, m ^ 1) for m in range(MEMBERS)])


def to_neighbour(x, by):
    return lax.ppermute(
        x, "member", [(m, (m + 2 * (by if m % 2 == 0 else -by)) % MEMBERS) for m in range(MEMBERS)]
    )


def exchange(x, groups):
    return lax.all_to_all(
        x, "member", split_axis=0, concat_axis=0, tiled=True, axis_index_groups=groups
    )


def pick_kernel(q_ref, tok_ref, slot_ref, out_ref):
    step = pl.program_id(0)
    shape = (tok_ref.shape[0], slot_ref.shape[1])
    chosen = (lax.broadcasted_iota(jnp.int32, shape, 0) == slot_ref[...]).astype(BF)
    got = lax.dot_general(
        tok_ref[...], chosen, (((0,), (0,)), ((), ())), preferred_element_type=F32
    ).astype(BF)
    rows = got.shape[0] // 2
    chip = 2 * (step & 3) + ((step >> 2) ^ q_ref[0])

    @pl.when(step < NA)
    def _():
        for c in range(2):
            out_ref[step, c, 0:rows] = got[c * rows : (c + 1) * rows]

    @pl.when(step >= NA)
    def _():
        out_ref[((chip + 1) >> 1) & 3, 0, rows : 2 * rows] = got[:rows]
        out_ref[((chip + 7) >> 1) & 3, 1, rows : 2 * rows] = got[rows:]


def pick(q, tokens, slot_token, rows):
    slots = slot_token.shape[1]
    return pl.pallas_call(
        pick_kernel,
        grid_spec=pltpu.PrefetchScalarGridSpec(
            num_scalar_prefetch=1,
            grid=(2 * NA,),
            in_specs=[
                pl.BlockSpec(
                    (tokens.shape[0], 2 * rows),
                    lambda i, q: (0, 2 * (i & 3) + ((i >> 2) ^ q[0])),
                ),
                pl.BlockSpec((1, slots), lambda i, q: (0, 0)),
            ],
            out_specs=pl.BlockSpec((NA, 2, 2 * rows, slots), lambda i, q: (0, 0, 0, 0)),
        ),
        out_shape=jax.ShapeDtypeStruct((NA, 2, 2 * rows, slots), BF),
        compiler_params=pltpu.CompilerParams(vmem_limit_bytes=VMEM),
        name="pick",
    )(q, tokens, slot_token).reshape(2 * NA, 2 * rows, slots)


def parts_kernel(which_ref, x_ref, w_ref, out_ref):
    out_ref[0] = jnp.dot(w_ref[...], x_ref[0, 0], preferred_element_type=F32).astype(BF)


def parts(which, routed, weights):
    na, _, depth, slots = routed.shape
    ff = weights.shape[0]
    return pl.pallas_call(
        parts_kernel,
        grid_spec=pltpu.PrefetchScalarGridSpec(
            num_scalar_prefetch=1,
            grid=(na,),
            in_specs=[
                pl.BlockSpec((1, 1, depth, slots), lambda i, which: (i, which[0], 0, 0)),
                pl.BlockSpec((ff, depth), lambda i, which: (0, 0)),
            ],
            out_specs=pl.BlockSpec((1, ff, slots), lambda i, which: (i, 0, 0)),
        ),
        out_shape=jax.ShapeDtypeStruct((na, ff, slots), BF),
        compiler_params=pltpu.CompilerParams(vmem_limit_bytes=VMEM),
        cost_estimate=pl.CostEstimate(
            flops=2 * na * ff * depth * slots,
            bytes_accessed=2 * (na * depth * slots + ff * depth + na * ff * slots),
            transcendentals=0,
        ),
        name="parts",
    )(which, routed, weights)


def hidden_kernel(scale, p_ref, cot_ref, out_ref):
    total = p_ref[0].astype(F32)
    for a in range(1, p_ref.shape[0]):
        total += p_ref[a].astype(F32)
    ff, slots = total.shape
    total = total.reshape(NX, NY, ff // (NX * NY), slots)
    total = jnp.concatenate([total[x, y] for y in range(NY) for x in range(NX)], axis=0)
    pre = total.T * scale
    sig = 1.0 / (1.0 + jnp.exp(-pre))
    grad = sig * (1.0 + pre * (1.0 - sig))
    hid = (cot_ref[...].astype(F32) * grad).astype(BF)
    for a in range(out_ref.shape[0]):
        out_ref[a] = hid


def hidden(partial, cot, scale):
    na, ff, slots = partial.shape
    return pl.pallas_call(
        lambda *refs: hidden_kernel(scale, *refs),
        in_specs=[pl.BlockSpec(memory_space=pltpu.VMEM)] * 2,
        out_specs=pl.BlockSpec(memory_space=pltpu.VMEM),
        out_shape=jax.ShapeDtypeStruct((na, slots, ff), BF),
        compiler_params=pltpu.CompilerParams(vmem_limit_bytes=VMEM),
        name="hidden",
    )(partial, cot)


def grad_kernel(which_ref, xm_ref, xo_ref, hm_ref, ho_ref, out_ref, acc_ref):
    step = pl.program_id(0)
    left = jnp.concatenate([xm_ref[0, 0, 0], xo_ref[0, 0, 0]], axis=1)
    right = jnp.concatenate([hm_ref[0], ho_ref[0]], axis=0)
    part = jnp.dot(left, right, preferred_element_type=F32)

    @pl.when(step == 0)
    def _():
        acc_ref[...] = part

    @pl.when(step > 0)
    def _():
        acc_ref[...] += part

    @pl.when(step == pl.num_programs(0) - 1)
    def _():
        out_ref[...] = acc_ref[...].astype(out_ref.dtype)


def team_grad(which, block, routed, hid_mine, hid_other, dtype):
    na, _, _, rows, slots = routed.shape
    ff = hid_mine.shape[2]
    return pl.pallas_call(
        grad_kernel,
        grid_spec=pltpu.PrefetchScalarGridSpec(
            num_scalar_prefetch=1,
            grid=(na,),
            in_specs=[
                pl.BlockSpec((1, 1, 1, rows, slots), lambda i, w: (i, w[0], block, 0, 0)),
                pl.BlockSpec((1, 1, 1, rows, slots), lambda i, w: (i, 1 - w[0], block, 0, 0)),
                pl.BlockSpec((1, slots, ff), lambda i, w: (i, 0, 0)),
                pl.BlockSpec((1, slots, ff), lambda i, w: (i, 0, 0)),
            ],
            out_specs=pl.BlockSpec((rows, ff), lambda i, w: (0, 0)),
            scratch_shapes=[pltpu.VMEM((rows, ff), F32)],
        ),
        out_shape=jax.ShapeDtypeStruct((rows, ff), dtype),
        compiler_params=pltpu.CompilerParams(vmem_limit_bytes=VMEM),
        cost_estimate=pl.CostEstimate(
            flops=4 * na * rows * slots * ff,
            bytes_accessed=4 * na * slots * (rows + ff) + 4 * rows * ff,
            transcendentals=0,
        ),
        name="team_grad",
    )(which, routed, routed, hid_mine, hid_other)


def pack(x):
    tail = x[:, :, 256:]
    pad = jnp.zeros_like(tail[:, :8])
    return jnp.concatenate(
        [
            x[:, :, :128],
            x[:, :, 128:256],
            jnp.concatenate([tail[:, :8], tail[:, 8:16]], axis=2),
            jnp.concatenate([tail[:, 16:], pad], axis=2),
        ],
        axis=1,
    )


def unpack(x):
    tail = jnp.concatenate([x[48:56, :64], x[48:56, 64:], x[56:, :64]], axis=0)
    return jnp.concatenate([x[:24], x[24:48], tail], axis=1)


def step_kernel(scale, cols, own_ref, far_ref, m1_ref, m2_ref, err_ref, out_ref):
    grad = (own_ref[...] + far_ref[...].astype(F32)) * scale
    one = 0.9 * m1_ref[...] + 0.1 * grad
    two = 0.95 * m2_ref[...] + 0.05 * grad * grad
    moved = 0.25 * (one / (jnp.sqrt(two) + 1e-08)) + err_ref[...].astype(F32)
    out_ref[...] = pack(moved.T.reshape(-1, cols, moved.shape[0])).astype(BF)


def inner_step(own, far, m1, m2, err, scale, cols):
    rows, ff = own.shape
    blk = ff // 2
    spec = pl.BlockSpec((rows, blk), lambda i: (0, i))
    return pl.pallas_call(
        lambda *refs: step_kernel(scale, cols, *refs),
        grid=(ff // blk,),
        in_specs=[spec] * 5,
        out_specs=pl.BlockSpec((blk // cols, PACKED, 128), lambda i: (i, 0, 0)),
        out_shape=jax.ShapeDtypeStruct((ff // cols, PACKED, 128), BF),
        compiler_params=pltpu.CompilerParams(vmem_limit_bytes=VMEM),
        name="inner_step",
    )(own, far, m1, m2, err)


def local(
    tokens,
    cotangent,
    slot_token,
    outer_weight,
    outer_momentum,
    first_moment,
    second_moment,
    error_state,
):
    scale = float(tokens.shape[2]) ** (-0.5)
    rows, cols = outer_weight.shape
    slots = slot_token.shape[1]
    weight_t = outer_weight.T
    member = lax.axis_index("member")
    core = member & 1
    q = (member >> 1) & 1
    mine = core.astype(jnp.int32).reshape(1)
    other = 1 - mine

    picked = pick(q.reshape(1), tokens[0], slot_token, rows)

    low = weight_t.astype(BF)
    low = jnp.concatenate([low, to_neighbour(low, 1)], axis=1)
    picked, low = lax.optimization_barrier((picked, low))
    near = lax.ppermute(low, "island", [(i, i ^ NX) for i in range(NX * NY)])
    routed = exchange(picked, TEAM).reshape(NA, 2, 2 * rows, slots)
    y = lax.axis_index("island") >> 2
    odd = (y & 1) == 1
    pair = jnp.where(odd, jnp.stack([near, low]), jnp.stack([low, near]))
    ring = [pair] + [
        lax.ppermute(
            pair,
            "island",
            [(i, (i + 2 * NX * k) % (NX * NY)) for i in range(NX * NY)],
        )
        for k in (1, 2, 3)
    ]
    ring = jnp.stack([ring[k] for k in (0, 3, 2, 1, 0, 3, 2, 1)])
    column = lax.dynamic_slice_in_dim(ring, (4 - (y >> 1)) & 3, 4, axis=0)
    weights = lax.all_gather(
        column.reshape(NY * cols, 2 * rows), "island", axis=0, tiled=True, axis_index_groups=ALONG_X
    )

    sent = swap(parts(other, routed, weights))
    kept = parts(mine, routed, weights)
    summed = (kept.astype(F32) + sent.astype(F32)).astype(BF)
    hid = hidden(exchange(summed, SAME_CORE), cotangent[0], scale)
    hid_mine = exchange(hid, SAME_CORE)
    hid_other = swap(hid_mine)

    routed = routed.reshape(NA, 2, 2, rows, slots)
    far = to_neighbour(team_grad(mine, 1, routed, hid_mine, hid_other, BF), -1)
    own = team_grad(mine, 0, routed, hid_mine, hid_other, F32)
    moved = inner_step(own, far, first_moment[0], second_moment[0], error_state[0], scale, cols)
    shares = lax.all_to_all(
        moved, "island", split_axis=0, concat_axis=0, tiled=True
    )
    averaged = unpack(jnp.sum(shares.astype(F32), axis=0)) / float(NX * NY) + 0.025 * weight_t
    new_momentum = 0.9 * outer_momentum.T + averaged
    new_outer = weight_t - 0.7 * (averaged + 0.9 * new_momentum)
    return (new_outer.T, new_momentum.T)


def solution(mesh):
    in_specs = (
        P("island", "member", None),
        P("island", "member", None),
        P("island", "member"),
        P("member", "island"),
        P("member", "island"),
        P("island", "member", None),
        P("island", "member", None),
        P("island", "member", None),
    )
    out_specs = (P("member", "island"), P("member", "island"))
    return jax.shard_map(local, mesh=mesh, in_specs=in_specs, out_specs=out_specs, check_vma=False)
```

```python
import jax
import jax.numpy as jnp
from jax import lax
from jax.experimental import pallas as pl
from jax.experimental.pallas import tpu as pltpu
from jax.sharding import PartitionSpec as P

NY, NX, NA = 8, 4, 4
ALONG_X = [[y * NX + x for x in range(NX)] for y in range(NY)]
PAIRS = [[(2 * p + b) * NX + x for p in range(NY // 2)] for b in range(2) for x in range(NX)]
TEAM = [[4 * a + 2 * q + c for a in range(NA) for c in range(2)] for q in range(2)]
SAME_CORE = [[4 * a + 2 * q + c for a in range(NA)] for q in range(2) for c in range(2)]
MEMBERS = 4 * NA
BF = jnp.bfloat16
F32 = jnp.float32
VMEM = 16 * 2**20
PACKED = 64
WHOLE = pl.BlockSpec(memory_space=pltpu.VMEM)


def swap(x):
    return lax.ppermute(x, "member", [(m, m ^ 1) for m in range(MEMBERS)])


def to_neighbour(x, by):
    return lax.ppermute(
        x, "member", [(m, (m + 2 * (by if m % 2 == 0 else -by)) % MEMBERS) for m in range(MEMBERS)]
    )


def exchange(x, groups):
    return lax.all_to_all(
        x, "member", split_axis=0, concat_axis=0, tiled=True, axis_index_groups=groups
    )


def pick_kernel(q_ref, tok_ref, slot_ref, out_ref):
    step = pl.program_id(0)
    shape = (tok_ref.shape[0], slot_ref.shape[1])
    chosen = (lax.broadcasted_iota(jnp.int32, shape, 0) == slot_ref[...]).astype(BF)
    got = lax.dot_general(
        tok_ref[...], chosen, (((0,), (0,)), ((), ())), preferred_element_type=F32
    ).astype(BF)
    rows = got.shape[0] // 2
    chip = 2 * (step & 3) + ((step >> 2) ^ q_ref[0])

    @pl.when(step < NA)
    def _():
        for c in range(2):
            out_ref[step, c, 0:rows] = got[c * rows : (c + 1) * rows]

    @pl.when(step >= NA)
    def _():
        out_ref[((chip + 1) >> 1) & 3, 0, rows : 2 * rows] = got[:rows]
        out_ref[((chip + 7) >> 1) & 3, 1, rows : 2 * rows] = got[rows:]


def pick(q, tokens, slot_token, rows):
    slots = slot_token.shape[1]
    return pl.pallas_call(
        pick_kernel,
        grid_spec=pltpu.PrefetchScalarGridSpec(
            num_scalar_prefetch=1,
            grid=(2 * NA,),
            in_specs=[
                pl.BlockSpec(
                    (tokens.shape[0], 2 * rows),
                    lambda i, q: (0, 2 * (i & 3) + ((i >> 2) ^ q[0])),
                ),
                pl.BlockSpec((1, slots), lambda i, q: (0, 0)),
            ],
            out_specs=pl.BlockSpec((NA, 2, 2 * rows, slots), lambda i, q: (0, 0, 0, 0)),
        ),
        out_shape=jax.ShapeDtypeStruct((NA, 2, 2 * rows, slots), BF),
        compiler_params=pltpu.CompilerParams(vmem_limit_bytes=VMEM),
        name="pick",
    )(q, tokens, slot_token).reshape(2 * NA, 2 * rows, slots)


def parts_kernel(which_ref, x_ref, w_ref, out_ref):
    for a in range(x_ref.shape[0]):
        out_ref[a] = jnp.dot(
            w_ref[...], x_ref[a, which_ref[0]], preferred_element_type=F32
        ).astype(BF)


def parts(which, routed, weights):
    na, _, depth, slots = routed.shape
    ff = weights.shape[0]
    return pl.pallas_call(
        parts_kernel,
        in_specs=[pl.BlockSpec(memory_space=pltpu.SMEM)] + [WHOLE] * 2,
        out_specs=WHOLE,
        out_shape=jax.ShapeDtypeStruct((na, ff, slots), BF),
        compiler_params=pltpu.CompilerParams(vmem_limit_bytes=VMEM),
        cost_estimate=pl.CostEstimate(
            flops=2 * na * ff * depth * slots,
            bytes_accessed=2 * (na * depth * slots + ff * depth + na * ff * slots),
            transcendentals=0,
        ),
        name="parts",
    )(which, routed, weights)


def hidden_kernel(scale, p_ref, cot_ref, out_ref):
    total = p_ref[0].astype(F32)
    for a in range(1, p_ref.shape[0]):
        total += p_ref[a].astype(F32)
    ff, slots = total.shape
    total = total.reshape(NX, NY, ff // (NX * NY), slots)
    total = jnp.concatenate([total[x, y] for y in range(NY) for x in range(NX)], axis=0)
    pre = total.T * scale
    sig = 1.0 / (1.0 + jnp.exp(-pre))
    grad = sig * (1.0 + pre * (1.0 - sig))
    hid = (cot_ref[...].astype(F32) * grad).astype(BF)
    for a in range(out_ref.shape[0]):
        out_ref[a] = hid


def hidden(partial, cot, scale):
    na, ff, slots = partial.shape
    return pl.pallas_call(
        lambda *refs: hidden_kernel(scale, *refs),
        in_specs=[WHOLE] * 2,
        out_specs=WHOLE,
        out_shape=jax.ShapeDtypeStruct((na, slots, ff), BF),
        compiler_params=pltpu.CompilerParams(vmem_limit_bytes=VMEM),
        name="hidden",
    )(partial, cot)


def grad_kernel(block, which_ref, x_ref, hm_ref, ho_ref, out_ref):
    core = which_ref[0]
    na = x_ref.shape[0]
    left = jnp.concatenate(
        [x_ref[a, c, block] for a in range(na) for c in (core, 1 - core)], axis=1
    )
    for k in range(0, out_ref.shape[1], 256):
        right = jnp.concatenate(
            [h[a, :, k : k + 256] for a in range(na) for h in (hm_ref, ho_ref)], axis=0
        )
        out_ref[:, k : k + 256] = jnp.dot(left, right, preferred_element_type=F32).astype(
            out_ref.dtype
        )


def team_grad(which, block, routed, hid_mine, hid_other, dtype):
    na, _, _, rows, slots = routed.shape
    ff = hid_mine.shape[2]
    return pl.pallas_call(
        lambda *refs: grad_kernel(block, *refs),
        in_specs=[pl.BlockSpec(memory_space=pltpu.SMEM)] + [WHOLE] * 3,
        out_specs=WHOLE,
        out_shape=jax.ShapeDtypeStruct((rows, ff), dtype),
        compiler_params=pltpu.CompilerParams(vmem_limit_bytes=VMEM),
        cost_estimate=pl.CostEstimate(
            flops=4 * na * rows * slots * ff,
            bytes_accessed=4 * na * slots * (rows + ff) + 4 * rows * ff,
            transcendentals=0,
        ),
        name="team_grad",
    )(which, routed, hid_mine, hid_other)


def pack(x):
    tail = x[:, :, 256:]
    pad = jnp.zeros_like(tail[:, :8])
    return jnp.concatenate(
        [
            x[:, :, :128],
            x[:, :, 128:256],
            jnp.concatenate([tail[:, :8], tail[:, 8:16]], axis=2),
            jnp.concatenate([tail[:, 16:], pad], axis=2),
        ],
        axis=1,
    )


def unpack(x):
    tail = jnp.concatenate([x[48:56, :64], x[48:56, 64:], x[56:, :64]], axis=0)
    return jnp.concatenate([x[:24], x[24:48], tail], axis=1)


def step_kernel(scale, cols, own_ref, far_ref, m1_ref, m2_ref, err_ref, out_ref):
    rows, ff = own_ref.shape
    wide = 16 * cols
    for k in range(0, ff, wide):
        at = slice(k, k + wide)
        grad = (own_ref[:, at] + far_ref[:, at].astype(F32)) * scale
        one = 0.9 * m1_ref[:, at] + 0.1 * grad
        two = 0.95 * m2_ref[:, at] + 0.05 * grad * grad
        moved = 0.25 * (one / (jnp.sqrt(two) + 1e-08)) + err_ref[:, at].astype(F32)
        out_ref[k // cols : (k + wide) // cols] = pack(moved.T.reshape(-1, cols, rows)).astype(BF)


def inner_step(own, far, m1, m2, err, scale, cols):
    ff = own.shape[1]
    return pl.pallas_call(
        lambda *refs: step_kernel(scale, cols, *refs),
        in_specs=[WHOLE] * 5,
        out_specs=WHOLE,
        out_shape=jax.ShapeDtypeStruct((ff // cols, PACKED, 128), BF),
        compiler_params=pltpu.CompilerParams(vmem_limit_bytes=VMEM),
        name="inner_step",
    )(own, far, m1, m2, err)


def local(
    tokens,
    cotangent,
    slot_token,
    outer_weight,
    outer_momentum,
    first_moment,
    second_moment,
    error_state,
):
    scale = float(tokens.shape[2]) ** (-0.5)
    rows, cols = outer_weight.shape
    slots = slot_token.shape[1]
    weight_t = outer_weight.T
    member = lax.axis_index("member")
    core = member & 1
    q = (member >> 1) & 1
    mine = core.astype(jnp.int32).reshape(1)
    other = 1 - mine

    picked = pick(q.reshape(1), tokens[0], slot_token, rows)

    low = weight_t.astype(BF)
    low = jnp.concatenate([low, to_neighbour(low, 1)], axis=1)
    picked, low = lax.optimization_barrier((picked, low))
    near = lax.ppermute(low, "island", [(i, i ^ NX) for i in range(NX * NY)])
    routed = exchange(picked, TEAM).reshape(NA, 2, 2 * rows, slots)
    y = lax.axis_index("island") >> 2
    odd = (y & 1) == 1
    pair = jnp.where(odd, jnp.stack([near, low]), jnp.stack([low, near]))
    column = lax.all_gather(
        pair.reshape(2 * cols, 2 * rows), "island", axis=0, tiled=True, axis_index_groups=PAIRS
    )
    weights = lax.all_gather(
        column, "island", axis=0, tiled=True, axis_index_groups=ALONG_X
    )

    sent = swap(parts(other, routed, weights))
    kept = parts(mine, routed, weights)
    summed = (kept.astype(F32) + sent.astype(F32)).astype(BF)
    hid = hidden(exchange(summed, SAME_CORE), cotangent[0], scale)
    hid_mine = exchange(hid, SAME_CORE)
    hid_other = swap(hid_mine)

    routed = routed.reshape(NA, 2, 2, rows, slots)
    far = to_neighbour(team_grad(mine, 1, routed, hid_mine, hid_other, BF), -1)
    own = team_grad(mine, 0, routed, hid_mine, hid_other, F32)
    moved = inner_step(own, far, first_moment[0], second_moment[0], error_state[0], scale, cols)
    shares = lax.all_to_all(
        moved, "island", split_axis=0, concat_axis=0, tiled=True
    )
    averaged = unpack(jnp.sum(shares.astype(F32), axis=0)) / float(NX * NY) + 0.025 * weight_t
    new_momentum = 0.9 * outer_momentum.T + averaged
    new_outer = weight_t - 0.7 * (averaged + 0.9 * new_momentum)
    return (new_outer.T, new_momentum.T)


def solution(mesh):
    in_specs = (
        P("island", "member", None),
        P("island", "member", None),
        P("island", "member"),
        P("member", "island"),
        P("member", "island"),
        P("island", "member", None),
        P("island", "member", None),
        P("island", "member", None),
    )
    out_specs = (P("member", "island"), P("member", "island"))
    return jax.shard_map(local, mesh=mesh, in_specs=in_specs, out_specs=out_specs, check_vma=False)
```

```python
import jax
import jax.numpy as jnp
from jax import lax
from jax.experimental import pallas as pl
from jax.experimental.pallas import tpu as pltpu
from jax.sharding import PartitionSpec as P

NY, NX, NA = 8, 4, 4
ALONG_X = [[y * NX + x for x in range(NX)] for y in range(NY)]
PAIRS = [[(2 * p + b) * NX + x for p in range(NY // 2)] for b in range(2) for x in range(NX)]
TEAM = [[4 * a + 2 * q + c for a in range(NA) for c in range(2)] for q in range(2)]
SAME_CORE = [[4 * a + 2 * q + c for a in range(NA)] for q in range(2) for c in range(2)]
MEMBERS = 4 * NA
BF = jnp.bfloat16
F32 = jnp.float32
VMEM = 16 * 2**20
PACKED = 64
PIECES = 2
WHOLE = pl.BlockSpec(memory_space=pltpu.VMEM)


def swap(x):
    return lax.ppermute(x, "member", [(m, m ^ 1) for m in range(MEMBERS)])


def to_neighbour(x, by):
    return lax.ppermute(
        x, "member", [(m, (m + 2 * (by if m % 2 == 0 else -by)) % MEMBERS) for m in range(MEMBERS)]
    )


def exchange(x, groups):
    return lax.all_to_all(
        x, "member", split_axis=0, concat_axis=0, tiled=True, axis_index_groups=groups
    )


def pick_kernel(q_ref, tok_ref, slot_ref, out_ref, held, slots, sems):
    parts, tokens, wide = held.shape
    rows = out_ref.shape[2] // 2
    fetched = [pltpu.make_async_copy(slot_ref, slots, sems.at[parts])]
    for p in range(parts):
        source = tok_ref.at[:, p * wide : (p + 1) * wide]
        fetched.append(pltpu.make_async_copy(source, held.at[p], sems.at[p]))
    for copy in fetched:
        copy.start()
    fetched[0].wait()
    chosen = (lax.broadcasted_iota(jnp.int32, (tokens, slots.shape[1]), 0) == slots[...]).astype(BF)
    for p in range(parts):
        fetched[p + 1].wait()
        got = lax.dot_general(
            held[p], chosen, (((0,), (0,)), ((), ())), preferred_element_type=F32
        ).astype(BF)
        for k in range(0, wide, 2 * rows):
            w = (p * wide + k) // (2 * rows)
            own = q_ref[0] == w % 2
            at = pl.ds(pl.multiple_of(jnp.where(own, 0, rows), rows), rows)
            below = jnp.where(own, w // 2, (w + 1) // 2 % NA)
            above = jnp.where(own, w // 2, (w + 7) // 2 % NA)
            out_ref[below, 0, at] = got[k : k + rows]
            out_ref[above, 1, at] = got[k + rows : k + 2 * rows]


def pick(q, tokens, slot_token, rows):
    slots = slot_token.shape[1]
    return pl.pallas_call(
        pick_kernel,
        in_specs=[pl.BlockSpec(memory_space=pltpu.SMEM)] + [pl.BlockSpec(memory_space=pl.ANY)] * 2,
        out_specs=WHOLE,
        out_shape=jax.ShapeDtypeStruct((NA, 2, 2 * rows, slots), BF),
        scratch_shapes=[
            pltpu.VMEM((PIECES, tokens.shape[0], tokens.shape[1] // PIECES), BF),
            pltpu.VMEM((1, slots), jnp.int32),
            pltpu.SemaphoreType.DMA((PIECES + 1,)),
        ],
        compiler_params=pltpu.CompilerParams(vmem_limit_bytes=60 * 2**20),
        name="pick",
    )(q, tokens, slot_token).reshape(2 * NA, 2 * rows, slots)


def parts_kernel(which_ref, x_ref, w_ref, out_ref):
    for a in range(x_ref.shape[0]):
        out_ref[a] = jnp.dot(
            w_ref[...], x_ref[a, which_ref[0]], preferred_element_type=F32
        ).astype(BF)


def parts(which, routed, weights):
    na, _, depth, slots = routed.shape
    ff = weights.shape[0]
    return pl.pallas_call(
        parts_kernel,
        in_specs=[pl.BlockSpec(memory_space=pltpu.SMEM)] + [WHOLE] * 2,
        out_specs=WHOLE,
        out_shape=jax.ShapeDtypeStruct((na, ff, slots), BF),
        compiler_params=pltpu.CompilerParams(vmem_limit_bytes=VMEM),
        cost_estimate=pl.CostEstimate(
            flops=2 * na * ff * depth * slots,
            bytes_accessed=2 * (na * depth * slots + ff * depth + na * ff * slots),
            transcendentals=0,
        ),
        name="parts",
    )(which, routed, weights)


def hidden_kernel(scale, p_ref, cot_ref, out_ref):
    total = p_ref[0].astype(F32)
    for a in range(1, p_ref.shape[0]):
        total += p_ref[a].astype(F32)
    ff, slots = total.shape
    total = total.reshape(NX, NY, ff // (NX * NY), slots)
    total = jnp.concatenate([total[x, y] for y in range(NY) for x in range(NX)], axis=0)
    pre = total.T * scale
    sig = 1.0 / (1.0 + jnp.exp(-pre))
    grad = sig * (1.0 + pre * (1.0 - sig))
    hid = (cot_ref[...].astype(F32) * grad).astype(BF)
    for a in range(out_ref.shape[0]):
        out_ref[a] = hid


def hidden(partial, cot, scale):
    na, ff, slots = partial.shape
    return pl.pallas_call(
        lambda *refs: hidden_kernel(scale, *refs),
        in_specs=[WHOLE] * 2,
        out_specs=WHOLE,
        out_shape=jax.ShapeDtypeStruct((na, slots, ff), BF),
        compiler_params=pltpu.CompilerParams(vmem_limit_bytes=VMEM),
        name="hidden",
    )(partial, cot)


def grad_kernel(block, which_ref, x_ref, hm_ref, ho_ref, out_ref):
    core = which_ref[0]
    na = x_ref.shape[0]
    left = jnp.concatenate(
        [x_ref[a, c, block] for a in range(na) for c in (core, 1 - core)], axis=1
    )
    for k in range(0, out_ref.shape[1], 256):
        right = jnp.concatenate(
            [h[a, :, k : k + 256] for a in range(na) for h in (hm_ref, ho_ref)], axis=0
        )
        out_ref[:, k : k + 256] = jnp.dot(left, right, preferred_element_type=F32).astype(
            out_ref.dtype
        )


def team_grad(which, block, routed, hid_mine, hid_other, dtype):
    na, _, _, rows, slots = routed.shape
    ff = hid_mine.shape[2]
    return pl.pallas_call(
        lambda *refs: grad_kernel(block, *refs),
        in_specs=[pl.BlockSpec(memory_space=pltpu.SMEM)] + [WHOLE] * 3,
        out_specs=WHOLE,
        out_shape=jax.ShapeDtypeStruct((rows, ff), dtype),
        compiler_params=pltpu.CompilerParams(vmem_limit_bytes=VMEM),
        cost_estimate=pl.CostEstimate(
            flops=4 * na * rows * slots * ff,
            bytes_accessed=4 * na * slots * (rows + ff) + 4 * rows * ff,
            transcendentals=0,
        ),
        name="team_grad",
    )(which, routed, hid_mine, hid_other)


def pack(x):
    tail = x[:, :, 256:]
    pad = jnp.zeros_like(tail[:, :8])
    return jnp.concatenate(
        [
            x[:, :, :128],
            x[:, :, 128:256],
            jnp.concatenate([tail[:, :8], tail[:, 8:16]], axis=2),
            jnp.concatenate([tail[:, 16:], pad], axis=2),
        ],
        axis=1,
    )


def unpack(x):
    tail = jnp.concatenate([x[48:56, :64], x[48:56, 64:], x[56:, :64]], axis=0)
    return jnp.concatenate([x[:24], x[24:48], tail], axis=1)


def step_kernel(scale, cols, own_ref, far_ref, m1_ref, m2_ref, err_ref, out_ref):
    rows, ff = own_ref.shape
    wide = 16 * cols
    for k in range(0, ff, wide):
        at = slice(k, k + wide)
        grad = (own_ref[:, at] + far_ref[:, at].astype(F32)) * scale
        one = 0.9 * m1_ref[:, at] + 0.1 * grad
        two = 0.95 * m2_ref[:, at] + 0.05 * grad * grad
        moved = 0.25 * (one / (jnp.sqrt(two) + 1e-08)) + err_ref[:, at].astype(F32)
        out_ref[k // cols : (k + wide) // cols] = pack(moved.T.reshape(-1, cols, rows)).astype(BF)


def inner_step(own, far, m1, m2, err, scale, cols):
    ff = own.shape[1]
    return pl.pallas_call(
        lambda *refs: step_kernel(scale, cols, *refs),
        in_specs=[WHOLE] * 5,
        out_specs=WHOLE,
        out_shape=jax.ShapeDtypeStruct((ff // cols, PACKED, 128), BF),
        compiler_params=pltpu.CompilerParams(vmem_limit_bytes=VMEM),
        name="inner_step",
    )(own, far, m1, m2, err)


def local(
    tokens,
    cotangent,
    slot_token,
    outer_weight,
    outer_momentum,
    first_moment,
    second_moment,
    error_state,
):
    scale = float(tokens.shape[2]) ** (-0.5)
    rows, cols = outer_weight.shape
    slots = slot_token.shape[1]
    weight_t = outer_weight.T
    member = lax.axis_index("member")
    core = member & 1
    q = (member >> 1) & 1
    mine = core.astype(jnp.int32).reshape(1)
    other = 1 - mine

    picked = pick(q.reshape(1), tokens[0], slot_token, rows)

    low = weight_t.astype(BF)
    low = jnp.concatenate([low, to_neighbour(low, 1)], axis=1)
    picked, low = lax.optimization_barrier((picked, low))
    near = lax.ppermute(low, "island", [(i, i ^ NX) for i in range(NX * NY)])
    routed = exchange(picked, TEAM).reshape(NA, 2, 2 * rows, slots)
    y = lax.axis_index("island") >> 2
    odd = (y & 1) == 1
    pair = jnp.where(odd, jnp.stack([near, low]), jnp.stack([low, near]))
    column = lax.all_gather(
        pair.reshape(2 * cols, 2 * rows), "island", axis=0, tiled=True, axis_index_groups=PAIRS
    )
    weights = lax.all_gather(
        column, "island", axis=0, tiled=True, axis_index_groups=ALONG_X
    )

    sent = swap(parts(other, routed, weights))
    kept = parts(mine, routed, weights)
    summed = (kept.astype(F32) + sent.astype(F32)).astype(BF)
    hid = hidden(exchange(summed, SAME_CORE), cotangent[0], scale)
    hid_mine = exchange(hid, SAME_CORE)
    hid_other = swap(hid_mine)

    routed = routed.reshape(NA, 2, 2, rows, slots)
    far = to_neighbour(team_grad(mine, 1, routed, hid_mine, hid_other, BF), -1)
    own = team_grad(mine, 0, routed, hid_mine, hid_other, F32)
    moved = inner_step(own, far, first_moment[0], second_moment[0], error_state[0], scale, cols)
    shares = lax.all_to_all(
        moved, "island", split_axis=0, concat_axis=0, tiled=True
    )
    averaged = unpack(jnp.sum(shares.astype(F32), axis=0)) / float(NX * NY) + 0.025 * weight_t
    new_momentum = 0.9 * outer_momentum.T + averaged
    new_outer = weight_t - 0.7 * (averaged + 0.9 * new_momentum)
    return (new_outer.T, new_momentum.T)


def solution(mesh):
    in_specs = (
        P("island", "member", None),
        P("island", "member", None),
        P("island", "member"),
        P("member", "island"),
        P("member", "island"),
        P("island", "member", None),
        P("island", "member", None),
        P("island", "member", None),
    )
    out_specs = (P("member", "island"), P("member", "island"))
    return jax.shard_map(local, mesh=mesh, in_specs=in_specs, out_specs=out_specs, check_vma=False)
```

```python
import jax
import jax.numpy as jnp
from jax import lax
from jax.experimental import pallas as pl
from jax.experimental.pallas import tpu as pltpu
from jax.sharding import PartitionSpec as P

NY, NX, NA = 8, 4, 4
ALONG_X = [[y * NX + x for x in range(NX)] for y in range(NY)]
PAIRS = [[(2 * p + b) * NX + x for p in range(NY // 2)] for b in range(2) for x in range(NX)]
TEAM = [[4 * a + 2 * q + c for a in range(NA) for c in range(2)] for q in range(2)]
SAME_CORE = [[4 * a + 2 * q + c for a in range(NA)] for q in range(2) for c in range(2)]
MEMBERS = 4 * NA
BF = jnp.bfloat16
F32 = jnp.float32
VMEM = 16 * 2**20
PACKED = 64
PIECES = 1
WHOLE = pl.BlockSpec(memory_space=pltpu.VMEM)


def swap(x):
    return lax.ppermute(x, "member", [(m, m ^ 1) for m in range(MEMBERS)])


def to_neighbour(x, by):
    return lax.ppermute(
        x, "member", [(m, (m + 2 * (by if m % 2 == 0 else -by)) % MEMBERS) for m in range(MEMBERS)]
    )


def exchange(x, groups):
    return lax.all_to_all(
        x, "member", split_axis=0, concat_axis=0, tiled=True, axis_index_groups=groups
    )


def pick_kernel(q_ref, tok_ref, slot_ref, out_ref, held, slots, sems):
    parts, tokens, wide = held.shape
    rows = out_ref.shape[2] // 2
    fetched = [pltpu.make_async_copy(slot_ref, slots, sems.at[parts])]
    for p in range(parts):
        source = tok_ref.at[:, p * wide : (p + 1) * wide]
        fetched.append(pltpu.make_async_copy(source, held.at[p], sems.at[p]))
    for copy in fetched:
        copy.start()
    fetched[0].wait()
    chosen = (lax.broadcasted_iota(jnp.int32, (tokens, slots.shape[1]), 0) == slots[...]).astype(BF)
    for p in range(parts):
        fetched[p + 1].wait()
        got = lax.dot_general(
            held[p], chosen, (((0,), (0,)), ((), ())), preferred_element_type=F32
        ).astype(BF)
        for k in range(0, wide, 2 * rows):
            w = (p * wide + k) // (2 * rows)
            own = q_ref[0] == w % 2
            at = pl.ds(pl.multiple_of(jnp.where(own, 0, rows), rows), rows)
            below = jnp.where(own, w // 2, (w + 1) // 2 % NA)
            above = jnp.where(own, w // 2, (w + 7) // 2 % NA)
            out_ref[below, 0, at] = got[k : k + rows]
            out_ref[above, 1, at] = got[k + rows : k + 2 * rows]


def pick(q, tokens, slot_token, rows):
    slots = slot_token.shape[1]
    return pl.pallas_call(
        pick_kernel,
        in_specs=[pl.BlockSpec(memory_space=pltpu.SMEM)] + [pl.BlockSpec(memory_space=pl.ANY)] * 2,
        out_specs=WHOLE,
        out_shape=jax.ShapeDtypeStruct((NA, 2, 2 * rows, slots), BF),
        scratch_shapes=[
            pltpu.VMEM((PIECES, tokens.shape[0], tokens.shape[1] // PIECES), BF),
            pltpu.VMEM((1, slots), jnp.int32),
            pltpu.SemaphoreType.DMA((PIECES + 1,)),
        ],
        compiler_params=pltpu.CompilerParams(vmem_limit_bytes=60 * 2**20),
        name="pick",
    )(q, tokens, slot_token).reshape(2 * NA, 2 * rows, slots)


def parts_kernel(which_ref, x_ref, w_ref, out_ref):
    for a in range(x_ref.shape[0]):
        out_ref[a] = jnp.dot(
            w_ref[...], x_ref[a, which_ref[0]], preferred_element_type=F32
        ).astype(BF)


def parts(which, routed, weights):
    na, _, depth, slots = routed.shape
    ff = weights.shape[0]
    return pl.pallas_call(
        parts_kernel,
        in_specs=[pl.BlockSpec(memory_space=pltpu.SMEM)] + [WHOLE] * 2,
        out_specs=WHOLE,
        out_shape=jax.ShapeDtypeStruct((na, ff, slots), BF),
        compiler_params=pltpu.CompilerParams(vmem_limit_bytes=VMEM),
        cost_estimate=pl.CostEstimate(
            flops=2 * na * ff * depth * slots,
            bytes_accessed=2 * (na * depth * slots + ff * depth + na * ff * slots),
            transcendentals=0,
        ),
        name="parts",
    )(which, routed, weights)


def hidden_kernel(scale, p_ref, cot_ref, out_ref):
    total = p_ref[0].astype(F32)
    for a in range(1, p_ref.shape[0]):
        total += p_ref[a].astype(F32)
    ff, slots = total.shape
    total = total.reshape(NX, NY, ff // (NX * NY), slots)
    total = jnp.concatenate([total[x, y] for y in range(NY) for x in range(NX)], axis=0)
    pre = total.T * scale
    sig = 1.0 / (1.0 + jnp.exp(-pre))
    grad = sig * (1.0 + pre * (1.0 - sig))
    hid = (cot_ref[...].astype(F32) * grad).astype(BF)
    for a in range(out_ref.shape[0]):
        out_ref[a] = hid


def hidden(partial, cot, scale):
    na, ff, slots = partial.shape
    return pl.pallas_call(
        lambda *refs: hidden_kernel(scale, *refs),
        in_specs=[WHOLE] * 2,
        out_specs=WHOLE,
        out_shape=jax.ShapeDtypeStruct((na, slots, ff), BF),
        compiler_params=pltpu.CompilerParams(vmem_limit_bytes=VMEM),
        name="hidden",
    )(partial, cot)


def grad_kernel(block, which_ref, x_ref, hm_ref, ho_ref, out_ref):
    core = which_ref[0]
    na = x_ref.shape[0]
    left = jnp.concatenate(
        [x_ref[a, c, block] for a in range(na) for c in (core, 1 - core)], axis=1
    )
    for k in range(0, out_ref.shape[1], 256):
        right = jnp.concatenate(
            [h[a, :, k : k + 256] for a in range(na) for h in (hm_ref, ho_ref)], axis=0
        )
        out_ref[:, k : k + 256] = jnp.dot(left, right, preferred_element_type=F32).astype(
            out_ref.dtype
        )


def team_grad(which, block, routed, hid_mine, hid_other, dtype):
    na, _, _, rows, slots = routed.shape
    ff = hid_mine.shape[2]
    return pl.pallas_call(
        lambda *refs: grad_kernel(block, *refs),
        in_specs=[pl.BlockSpec(memory_space=pltpu.SMEM)] + [WHOLE] * 3,
        out_specs=WHOLE,
        out_shape=jax.ShapeDtypeStruct((rows, ff), dtype),
        compiler_params=pltpu.CompilerParams(vmem_limit_bytes=VMEM),
        cost_estimate=pl.CostEstimate(
            flops=4 * na * rows * slots * ff,
            bytes_accessed=4 * na * slots * (rows + ff) + 4 * rows * ff,
            transcendentals=0,
        ),
        name="team_grad",
    )(which, routed, hid_mine, hid_other)


def pack(x):
    tail = x[:, :, 256:]
    pad = jnp.zeros_like(tail[:, :8])
    return jnp.concatenate(
        [
            x[:, :, :128],
            x[:, :, 128:256],
            jnp.concatenate([tail[:, :8], tail[:, 8:16]], axis=2),
            jnp.concatenate([tail[:, 16:], pad], axis=2),
        ],
        axis=1,
    )


def unpack(x):
    tail = jnp.concatenate([x[48:56, :64], x[48:56, 64:], x[56:, :64]], axis=0)
    return jnp.concatenate([x[:24], x[24:48], tail], axis=1)


def step_kernel(scale, cols, own_ref, far_ref, m1_ref, m2_ref, err_ref, out_ref):
    rows, ff = own_ref.shape
    wide = 16 * cols
    for k in range(0, ff, wide):
        at = slice(k, k + wide)
        grad = (own_ref[:, at] + far_ref[:, at].astype(F32)) * scale
        one = 0.9 * m1_ref[:, at] + 0.1 * grad
        two = 0.95 * m2_ref[:, at] + 0.05 * grad * grad
        moved = 0.25 * (one / (jnp.sqrt(two) + 1e-08)) + err_ref[:, at].astype(F32)
        out_ref[k // cols : (k + wide) // cols] = pack(moved.T.reshape(-1, cols, rows)).astype(BF)


def inner_step(own, far, m1, m2, err, scale, cols):
    ff = own.shape[1]
    return pl.pallas_call(
        lambda *refs: step_kernel(scale, cols, *refs),
        in_specs=[WHOLE] * 5,
        out_specs=WHOLE,
        out_shape=jax.ShapeDtypeStruct((ff // cols, PACKED, 128), BF),
        compiler_params=pltpu.CompilerParams(vmem_limit_bytes=VMEM),
        name="inner_step",
    )(own, far, m1, m2, err)


def local(
    tokens,
    cotangent,
    slot_token,
    outer_weight,
    outer_momentum,
    first_moment,
    second_moment,
    error_state,
):
    scale = float(tokens.shape[2]) ** (-0.5)
    rows, cols = outer_weight.shape
    slots = slot_token.shape[1]
    weight_t = outer_weight.T
    member = lax.axis_index("member")
    core = member & 1
    q = (member >> 1) & 1
    mine = core.astype(jnp.int32).reshape(1)
    other = 1 - mine

    picked = pick(q.reshape(1), tokens[0], slot_token, rows)

    far_t = to_neighbour(weight_t, 1)
    picked, far_t = lax.optimization_barrier((picked, far_t))
    low = jnp.concatenate([weight_t, far_t], axis=1).astype(BF)
    near = lax.ppermute(low, "island", [(i, i ^ NX) for i in range(NX * NY)])
    routed = exchange(picked, TEAM).reshape(NA, 2, 2 * rows, slots)
    y = lax.axis_index("island") >> 2
    odd = (y & 1) == 1
    pair = jnp.where(odd, jnp.stack([near, low]), jnp.stack([low, near]))
    column = lax.all_gather(
        pair.reshape(2 * cols, 2 * rows), "island", axis=0, tiled=True, axis_index_groups=PAIRS
    )
    weights = lax.all_gather(
        column, "island", axis=0, tiled=True, axis_index_groups=ALONG_X
    )

    sent = swap(parts(other, routed, weights))
    kept = parts(mine, routed, weights)
    summed = (kept.astype(F32) + sent.astype(F32)).astype(BF)
    hid = hidden(exchange(summed, SAME_CORE), cotangent[0], scale)
    hid_mine = exchange(hid, SAME_CORE)
    hid_other = swap(hid_mine)

    routed = routed.reshape(NA, 2, 2, rows, slots)
    far = to_neighbour(team_grad(mine, 1, routed, hid_mine, hid_other, BF), -1)
    own = team_grad(mine, 0, routed, hid_mine, hid_other, F32)
    moved = inner_step(own, far, first_moment[0], second_moment[0], error_state[0], scale, cols)
    shares = lax.all_to_all(
        moved, "island", split_axis=0, concat_axis=0, tiled=True
    )
    averaged = unpack(jnp.sum(shares.astype(F32), axis=0)) / float(NX * NY) + 0.025 * weight_t
    new_momentum = 0.9 * outer_momentum.T + averaged
    new_outer = weight_t - 0.7 * (averaged + 0.9 * new_momentum)
    return (new_outer.T, new_momentum.T)


def solution(mesh):
    in_specs = (
        P("island", "member", None),
        P("island", "member", None),
        P("island", "member"),
        P("member", "island"),
        P("member", "island"),
        P("island", "member", None),
        P("island", "member", None),
        P("island", "member", None),
    )
    out_specs = (P("member", "island"), P("member", "island"))
    return jax.shard_map(local, mesh=mesh, in_specs=in_specs, out_specs=out_specs, check_vma=False)
```
